256 devices in a mesh: chan: 8 (over z), win: 4 (over x), freq: 8 (over y, core).
Axes of the slice: x: 4, y: 4, z: 8, core: 2. Of those that a mesh axis runs over, the one named last changes fastest.
Arguments:
- spectrogram: bfloat16 [16384, 32, 1024], P('chan', 'win', 'freq'), may hold values from 0 to 200, as said below
- window_factor: bfloat16 [32, 128], P(('win', 'freq')), may hold values from 0.099609375 to 1
- freq_factor: bfloat16 [1024, 128], P('freq'), may hold values from 0.099609375 to 1
- channel_factor: float32 [16384, 128], P(('chan', 'win', 'freq')), may hold values from 0 to 0.06
Outputs:
- channel_out: float32 [16384, 128], P(('chan', 'win', 'freq'))
- column_scale: float32 [128], replicated
The draws below stay inside these ranges and needn't reach their ends.
Inputs may be any that keep to these rules, and one draw needn't show every extreme that they name: `spectrogram`: nonnegative.
All inputs are finite; a program needn't handle non-finite values.
Results may differ from the reference program's by a relative error of at most 0.0022.
Values may be sent and summed in bfloat16 or wider, within the bound.
No kernel may reach another device: no remote copies, remote signals or barrier semaphores. Data moves between devices by JAX's collectives and lax.ppermute only.
A program may use at most 64 MiB of HBM per device.

```python
import math
import jax
import jax.numpy as jnp
from jax import lax

RANK = 128
FREQS = 1024
CH_DEV = 2048
CHANNELS = 16384
WINDOWS = 32
N_CHAN = 8


def draw_spectrogram(key, part):
    key = jax.random.fold_in(key, 7)
    keys = jax.random.split(key, 7)
    chan_pos = jnp.arange(CHANNELS, dtype=jnp.float32)
    ramp = 1.0 + 2.0 * chan_pos / max(CHANNELS - 1, 1)
    chan_scale = jnp.exp(jax.random.uniform(keys[0], (CHANNELS,), jnp.float32, math.log(0.3), math.log(3.0)))
    period = jnp.exp(jax.random.uniform(keys[1], (CHANNELS,), jnp.float32, math.log(6.0), math.log(20.0)))
    phase = jax.random.uniform(keys[2], (CHANNELS,), jnp.float32, 0.0, 1.0)
    drift = jax.random.uniform(keys[3], (CHANNELS,), jnp.float32, -0.3, 0.3)
    level = jnp.exp(jax.random.uniform(keys[4], (CHANNELS, WINDOWS), jnp.float32, math.log(0.05), math.log(8.0)))
    freq_scale = jnp.exp(jax.random.uniform(keys[5], (FREQS,), jnp.float32, math.log(0.3), math.log(3.0)))
    cell = jax.random.uniform(keys[6], (CHANNELS, WINDOWS, FREQS), jnp.float32, 0.5, 1.5)
    bins = jnp.arange(FREQS, dtype=jnp.float32)
    slots = jnp.arange(WINDOWS, dtype=jnp.float32)
    turns = bins[None, None, :] / period[:, None, None] - phase[:, None, None] - drift[:, None, None] * slots[None, :, None]
    comb = jnp.exp(4.0 * (jnp.cos(2.0 * math.pi * jnp.mod(turns, 1.0)) - 1.0))
    spectrum = 0.1 * freq_scale[None, None, :] + level[:, :, None] * comb
    values = (ramp * chan_scale)[:, None, None] * spectrum * cell
    return values.astype(jnp.bfloat16)


def block_levels(key, dims, cuts, low, largest):
    gain = 1.0
    for dim, shards_of in cuts:
        steps = jax.random.uniform(jax.random.fold_in(jax.random.fold_in(key, 6), dim), (shards_of,), jnp.float32, low / len(cuts), largest / len(cuts))
        gain = gain * jnp.repeat(jnp.exp(steps), dims[dim] // shards_of).reshape((-1,) + (1,) * (len(dims) - 1 - dim))
    return gain


def setup_inputs(seed: int = 0) -> dict:
    arg_keys = jax.random.split(jax.random.key(seed), 5)
    return {
        "spectrogram": draw_spectrogram(jax.random.fold_in(arg_keys[4], 71), 0),
        "window_factor": jnp.clip(0.099609375 + 0.9003906 * jax.random.uniform(arg_keys[1], (WINDOWS, RANK), jnp.float32) ** block_levels(arg_keys[1], (WINDOWS, RANK), ((0, 32),), -0.2, 0.2), 0.099609375, 1.0).astype(jnp.bfloat16),
        "freq_factor": jnp.clip(0.099609375 + 0.9003906 * jax.random.uniform(arg_keys[2], (FREQS, RANK), jnp.float32) ** block_levels(arg_keys[2], (FREQS, RANK), ((0, 8),), -0.2, 0.2), 0.099609375, 1.0).astype(jnp.bfloat16),
        "channel_factor": jnp.clip(0.06 * jax.random.uniform(arg_keys[3], (CHANNELS, RANK), jnp.float32) ** block_levels(arg_keys[3], (CHANNELS, RANK), ((0, 256),), -0.2, 0.2), 0.0, 0.06),
    }


def reference(spectrogram, window_factor, freq_factor, channel_factor):
    window_gram = jnp.dot(window_factor.T, window_factor, preferred_element_type=jnp.float32)
    freq_gram = jnp.dot(freq_factor.T, freq_factor, preferred_element_type=jnp.float32)
    gram = window_gram * freq_gram
    product = window_factor.astype(jnp.float32)[:, None, :] * freq_factor.astype(jnp.float32)[None, :, :]
    khatri_rao = product.astype(jnp.bfloat16).reshape(WINDOWS * FREQS, RANK)
    blocks = spectrogram.reshape(N_CHAN, CH_DEV, WINDOWS * FREQS)

    def contract(block):
        return jnp.dot(block, khatri_rao, preferred_element_type=jnp.float32)
    mttkrp = lax.map(contract, blocks).reshape(CHANNELS, RANK)

    def sweep(index, factor):
        old = lax.dynamic_slice_in_dim(factor, index, 1, 1)[:, 0]
        target = lax.dynamic_slice_in_dim(mttkrp, index, 1, 1)[:, 0]
        column = lax.dynamic_slice_in_dim(gram, index, 1, 1)[:, 0]
        pivot = lax.dynamic_slice(gram, (index, index), (1, 1))[0, 0]
        fitted = jnp.dot(factor, column, precision=lax.Precision.HIGHEST)
        fresh = jnp.maximum(old + (target - fitted) / pivot, 0.0)
        return lax.dynamic_update_slice_in_dim(factor, fresh[:, None], index, 1)
    updated = lax.fori_loop(0, RANK, sweep, channel_factor)
    column_scale = jnp.sqrt(lax.optimization_barrier(jnp.sum(updated * updated, axis=0)) / CHANNELS + 1e-06)
    return (updated / column_scale[None, :], column_scale)
```

```python
import jax
import jax.numpy as jnp
from jax import lax
from jax.experimental import pallas as pl
from jax.experimental.pallas import tpu as pltpu
from jax.sharding import Mesh, PartitionSpec as P

f32 = jnp.float32
DOWN = 0.125


def on_vmem(kernel, outs, *args):
    place = pl.BlockSpec(memory_space=pltpu.VMEM)
    return pl.pallas_call(
        kernel,
        out_shape=outs,
        in_specs=[place] * len(args),
        out_specs=jax.tree.map(lambda _: place, outs),
        compiler_params=pltpu.CompilerParams(vmem_limit_bytes=48 * 2**20),
    )(*args)


def swap(value, axis, distance):
    count = lax.axis_size(axis)
    return lax.ppermute(value, axis, [(i, i ^ distance) for i in range(count)])


def gram_kernel(own_ref, far_ref, window_ref, factor_ref, lower_ref, upper_ref, inverse_ref):
    def gram_of(block):
        return lax.dot_general(
            block, block, (((0,), (0,)), ((), ())), preferred_element_type=f32
        )

    rank = own_ref.shape[-1]
    gram = (gram_of(own_ref[...]) + gram_of(far_ref[...])) * gram_of(window_ref[...])
    row = lax.broadcasted_iota(jnp.int32, (rank, rank), 0)
    col = lax.broadcasted_iota(jnp.int32, (rank, rank), 1)
    inverse = 1.0 / jnp.sum(jnp.where(row == col, gram, 0.0), axis=1, keepdims=True)
    lower_ref[...] = jnp.where(row > col, gram, 0.0) * inverse
    upper = jnp.where(row < col, gram, 0.0) * inverse
    upper_ref[...] = lax.dot_general(
        upper,
        factor_ref[...],
        (((1,), (1,)), ((), ())),
        precision=lax.Precision.HIGHEST,
        preferred_element_type=f32,
    )
    inverse_ref[...] = jnp.broadcast_to(inverse, inverse_ref.shape)


def sweep_kernel(a_ref, b_ref, c_ref, d_ref, lower_ref, upper_ref, inverse_ref, out_ref, square_ref):
    mttkrp = (a_ref[...] + b_ref[...]) + (c_ref[...] + d_ref[...])
    start = mttkrp.T * inverse_ref[...] - upper_ref[...]
    rank, rows = start.shape
    parts = [start[8 * i : 8 * i + 8] for i in range(rank // 8)]
    for j in range(rank):
        block, lane = divmod(j, 8)
        fresh = jnp.maximum(parts[block], 0.0)[lane : lane + 1, :]
        fresh = jnp.broadcast_to(fresh, (8, rows))
        for i in range(block, rank // 8):
            column = jnp.broadcast_to(lower_ref[8 * i : 8 * i + 8, j : j + 1], (8, rows))
            parts[i] = parts[i] - column * fresh
    updated = jnp.maximum(jnp.concatenate(parts, axis=0), 0.0).T
    out_ref[...] = updated
    square_ref[...] = jnp.sum(updated * updated, axis=0, keepdims=True)


def body(spectrogram, window_factor, freq_factor, channel_factor):
    chan_rows, win_rows, freq_rows = spectrogram.shape
    rows, rank = channel_factor.shape
    xs, ys = lax.axis_size("x"), lax.axis_size("y")
    x, y, c = lax.axis_index("x"), lax.axis_index("y"), lax.axis_index("c")

    line = [window_factor] + [swap(window_factor, "y", k) for k in (1, 3, 2)]
    line = jnp.concatenate(line, axis=0)
    pair = swap(line, "c", 1)
    slot = jnp.arange(win_rows)[:, None]
    block = jnp.zeros((win_rows, rank), f32)
    for i, k in enumerate((0, 1, 3, 2)):
        block = jnp.where(slot == 2 * (y ^ k) + c, line[i : i + 1].astype(f32), block)
        block = jnp.where(slot == 2 * (y ^ k) + 1 - c, pair[i : i + 1].astype(f32), block)
    product = block[:, None, :] * freq_factor.astype(f32)[None, :, :]
    khatri_rao = product.astype(jnp.bfloat16).reshape(win_rows * freq_rows, rank)
    flat = spectrogram.reshape(chan_rows, win_rows * freq_rows)
    part = jnp.dot(flat, khatri_rao, preferred_element_type=f32)

    freqs = [freq_factor] + [swap(freq_factor, "y", k) for k in (1, 3, 2)]
    freqs = jnp.concatenate(freqs, axis=0)
    freqs_far = swap(freqs, "c", 1)
    block = block.astype(jnp.bfloat16)
    windows = jnp.concatenate([block] + [swap(block, "x", k) for k in (1, 3, 2)], axis=0)
    like = jax.ShapeDtypeStruct((rank, rows), f32)
    lower, upper, inverse = on_vmem(
        gram_kernel,
        (jax.ShapeDtypeStruct((rank, rank), f32), like, like),
        freqs,
        freqs_far,
        windows,
        channel_factor,
    )

    part = part.reshape(xs, ys, 2, rows, rank)
    mine = lax.dynamic_index_in_dim(part, c, 2, keepdims=False)
    other = lax.dynamic_index_in_dim(part, 1 - c, 2, keepdims=False)
    part = mine + swap(other, "c", 1)
    total = lax.dynamic_index_in_dim(part, y, 1, keepdims=False)
    small = (part * DOWN).astype(jnp.float16)
    for k in (1, 3, 2):
        piece = lax.dynamic_index_in_dim(small, y ^ k, 1, keepdims=False)
        total = total + swap(piece, "y", k).astype(f32) * (1.0 / DOWN)
    pieces = [lax.dynamic_index_in_dim(total, x, 0, keepdims=False)]
    for k in (1, 3, 2):
        piece = lax.dynamic_index_in_dim(total, x ^ k, 0, keepdims=False)
        pieces.append(swap(piece, "x", k))

    updated, squares = on_vmem(
        sweep_kernel,
        (jax.ShapeDtypeStruct((rows, rank), f32), jax.ShapeDtypeStruct((1, rank), f32)),
        *pieces,
        lower,
        upper,
        inverse,
    )
    squares = squares + swap(squares, "c", 1)
    chips = xs * ys * lax.axis_size("z")
    squares = lax.all_to_all(
        jnp.broadcast_to(squares, (chips, rank)), ("z", "x", "y"), 0, 0, tiled=True
    ).sum(axis=0)
    column_scale = jnp.sqrt(squares / (chips * 2 * rows) + 1e-06)
    return (updated / column_scale[None, :], column_scale)


def solution(mesh):
    chan, win, freq = mesh.devices.shape
    fine = Mesh(mesh.devices.reshape(chan, win, freq // 2, 2), ("z", "x", "y", "c"))
    placed = (
        P("z", "x", ("y", "c")),
        P(("x", "y", "c"), None),
        P(("y", "c"), None),
        P(("z", "x", "y", "c"), None),
    )
    return jax.shard_map(
        body,
        mesh=fine,
        in_specs=placed,
        out_specs=(P(("z", "x", "y", "c"), None), P()),
        check_vma=False,
    )
```

```python
import jax
import jax.numpy as jnp
from jax import lax
from jax.experimental import pallas as pl
from jax.experimental.pallas import tpu as pltpu
from jax.sharding import Mesh, PartitionSpec as P

f32, bf16, f16 = jnp.float32, jnp.bfloat16, jnp.float16
DOWN_C, DOWN_X, DOWN_Y = 1.0 / 4, 1.0 / 8, 1.0 / 32
NEAR = (2, 1, 3)
CHUNKS = 16
UP_U = 1024.0


def on_vmem(kernel, outs, *args, scratch=()):
    place = pl.BlockSpec(memory_space=pltpu.VMEM)
    return pl.pallas_call(
        kernel,
        out_shape=outs,
        in_specs=[place] * len(args),
        out_specs=jax.tree.map(lambda _: place, outs),
        scratch_shapes=scratch,
        compiler_params=pltpu.CompilerParams(vmem_limit_bytes=32 * 2**20),
    )(*args)


def swap(value, axis, distance):
    count = lax.axis_size(axis)
    return lax.ppermute(value, axis, [(i, i ^ distance) for i in range(count)])


def flatten_kernel(spectrogram_ref, other_ref, mine_ref, done_ref, buffer_ref, sem_ref):
    core = lax.axis_index("c")
    rows = spectrogram_ref.shape[0]
    chunk = other_ref.shape[0] // CHUNKS
    copies = []
    for side in range(2):
        for i in range(CHUNKS):
            offset = pl.multiple_of((2 * i + (core if side else 1 - core)) * chunk, chunk)
            copy = pltpu.make_async_copy(
                spectrogram_ref.at[pl.ds(offset, chunk)], buffer_ref.at[side, i], sem_ref.at[side, i]
            )
            copy.start()
            copies.append((side, i, copy))
    for side, i, copy in copies:
        copy.wait()
        out = mine_ref if side else other_ref
        out[chunk * i : chunk * (i + 1), :] = buffer_ref[side, i].reshape(chunk, out.shape[1])
    done_ref[...] = jnp.zeros_like(done_ref)


def lead_kernel(freq_ref, factor_ref, window_ref, out_ref, freq_out_ref, freq_buffer, factor_buffer, window_buffer, sem_ref):
    copies = [
        pltpu.make_async_copy(freq_ref, freq_buffer, sem_ref.at[0]),
        pltpu.make_async_copy(factor_ref, factor_buffer, sem_ref.at[1]),
        pltpu.make_async_copy(window_ref, window_buffer, sem_ref.at[2]),
    ]
    for copy in copies:
        copy.start()
    for copy in copies:
        copy.wait()
    freqs, rows = freq_ref.shape[0], factor_ref.shape[0]
    freq = freq_buffer[...]
    freq_out_ref[...] = freq
    out_ref[:freqs, :] = freq.astype(f32)
    out_ref[freqs : freqs + rows, :] = factor_buffer[...] * UP_U
    out_ref[freqs + rows :, :] = window_buffer[...].astype(f32)


def differ(part):
    lane = lax.broadcasted_iota(jnp.int32, part.shape, 1)
    return jnp.where(lane == 0, part, part - part[:, :1])


def other_kernel(flat_ref, block_ref, freq_ref, part_ref, khatri_rao_ref):
    freqs = freq_ref.shape[0]
    factor = freq_ref[...].astype(f32)
    for j in range(block_ref.shape[0]):
        khatri_rao_ref[freqs * j : freqs * (j + 1), :] = (block_ref[j : j + 1, :] * factor).astype(bf16)
    part_ref[...] = differ(jnp.dot(flat_ref[...], khatri_rao_ref[...], preferred_element_type=f32))


def mine_kernel(flat_ref, khatri_rao_ref, part_ref):
    part_ref[...] = differ(jnp.dot(flat_ref[...], khatri_rao_ref[...], preferred_element_type=f32))


def gram_of(block):
    return lax.dot_general(block, block, (((0,), (0,)), ((), ())), preferred_element_type=f32)


def gram_kernel(own_ref, far_ref, w0_ref, w1_ref, w2_ref, w3_ref, factor_ref, lower_ref, upper_ref, inverse_ref):
    rank = own_ref.shape[-1]

    def paired(blocks):
        own, two, one, three = (gram_of(v) for v in blocks)
        return (own + two) + (one + three)

    step = own_ref.shape[0] // 4
    freq = [paired([ref[step * i : step * (i + 1), :] for i in range(4)]) for ref in (own_ref, far_ref)]
    gram = (freq[0] + freq[1]) * paired([w[...] for w in (w0_ref, w1_ref, w2_ref, w3_ref)])
    row = lax.broadcasted_iota(jnp.int32, (rank, rank), 0)
    col = lax.broadcasted_iota(jnp.int32, (rank, rank), 1)
    inverse = 1.0 / jnp.sum(jnp.where(row == col, gram, 0.0), axis=1, keepdims=True)
    lower_ref[...] = jnp.where(row > col, gram, 0.0) * inverse
    upper = jnp.where(row < col, gram, 0.0) * inverse
    upper_ref[...] = lax.dot_general(
        upper,
        factor_ref[...],
        (((1,), (1,)), ((), ())),
        precision=lax.Precision.HIGHEST,
        preferred_element_type=f32,
    )
    inverse_ref[...] = jnp.broadcast_to(inverse, inverse_ref.shape)


def sweep_kernel(mttkrp_ref, lower_ref, upper_ref, inverse_ref, out_ref, square_ref):
    coded = mttkrp_ref[...].T * (1.0 / DOWN_Y)
    rank, rows = coded.shape
    row = lax.broadcasted_iota(jnp.int32, (rank, rows), 0)
    mttkrp = jnp.where(row == 0, coded, coded + coded[:1, :])
    start = mttkrp * inverse_ref[...] - upper_ref[...]
    parts = [start[8 * i : 8 * i + 8] for i in range(rank // 8)]
    for j in range(rank):
        block, lane = divmod(j, 8)
        fresh = jnp.maximum(parts[block], 0.0)[lane : lane + 1, :]
        fresh = jnp.broadcast_to(fresh, (8, rows))
        for i in range(block, rank // 8):
            column = jnp.broadcast_to(lower_ref[8 * i : 8 * i + 8, j : j + 1], (8, rows))
            parts[i] = parts[i] - column * fresh
    updated = jnp.maximum(jnp.concatenate(parts, axis=0), 0.0).T
    out_ref[...] = updated
    square_ref[...] = jnp.sum(updated * updated, axis=0, keepdims=True)


def body(spectrogram, window_factor, freq_factor, channel_factor):
    chan_rows, win_rows, freq_rows = spectrogram.shape
    rows, rank = channel_factor.shape
    xs, ys = lax.axis_size("x"), lax.axis_size("y")
    x, y, c = lax.axis_index("x"), lax.axis_index("y"), lax.axis_index("c")
    ux, uy = x.astype(jnp.uint32), y.astype(jnp.uint32)
    xs_near = [ux ^ jnp.uint32(k) for k in NEAR]
    own_slots = [2 * (y ^ k) + c for k in (0,) + NEAR]
    far_slots = [2 * (y ^ k) + 1 - c for k in (0,) + NEAR]
    from_near = [[(y ^ i) == k for k in NEAR] for i in range(ys)]
    uy_rows = uy * jnp.uint32(rows)

    lead = jnp.concatenate([freq_factor.astype(f32), channel_factor * UP_U, window_factor.astype(f32)], axis=0)
    lead = lax.optimization_barrier(lead)
    place = pl.BlockSpec(memory_space=pltpu.VMEM)
    high = lead.astype(f16)
    scaled = lead[freq_rows:-1]
    low = (scaled - scaled.astype(f16).astype(f32)).astype(f16)
    first = jnp.concatenate([high, low], axis=0)
    first, ux, xs_near, own_slots, far_slots, from_near, uy_rows = lax.optimization_barrier(
        (first, ux, xs_near, own_slots, far_slots, from_near, uy_rows)
    )
    first = [first] + [swap(first, "y", k) for k in NEAR]
    last = freq_rows + rows
    line = jnp.concatenate([v[last : last + 1] for v in first], axis=0)
    freqs = jnp.concatenate([v[:freq_rows] for v in first], axis=0).astype(bf16)
    olds = [v[freq_rows:last].astype(f32) + v[last + 1 :].astype(f32) for v in first]
    width = win_rows * freq_rows
    half = jax.ShapeDtypeStruct((chan_rows // 2, width), bf16)
    place = pl.BlockSpec(memory_space=pltpu.VMEM)
    flat_other, flat_mine, done = pl.pallas_call(
        flatten_kernel,
        out_shape=(half, half, jax.ShapeDtypeStruct((8, rank), f32)),
        in_specs=[pl.BlockSpec(memory_space=pl.ANY)],
        out_specs=(place, place, place),
        scratch_shapes=[
            pltpu.VMEM((2, CHUNKS, rows, win_rows, freq_rows), bf16),
            pltpu.SemaphoreType.DMA((2, CHUNKS)),
        ],
        compiler_params=pltpu.CompilerParams(vmem_limit_bytes=48 * 2**20),
        cost_estimate=pl.CostEstimate(flops=0, bytes_accessed=chan_rows * width * 4, transcendentals=0),
    )(spectrogram)
    line, freqs, done = lax.optimization_barrier((line, freqs, done))
    pair = swap(line, "c", 1)
    slot = jnp.arange(win_rows)[:, None]
    block = jnp.zeros((win_rows, rank), f32)
    for i in range(ys):
        block = jnp.where(slot == own_slots[i], line[i : i + 1].astype(f32), block)
        block = jnp.where(slot == far_slots[i], pair[i : i + 1].astype(f32), block)
    half = jax.ShapeDtypeStruct((chan_rows // 2, rank), f32)
    other, khatri_rao = on_vmem(
        other_kernel, (half, jax.ShapeDtypeStruct((width, rank), bf16)), flat_other, block, freq_factor
    )
    mine = on_vmem(mine_kernel, half, flat_mine, khatri_rao)

    far = swap((other * DOWN_C).astype(f16), "c", 1).astype(f32)
    part = (mine + far * (1.0 / DOWN_C)).reshape(xs, ys * rows, rank)
    total = lax.dynamic_index_in_dim(part, ux, 0, keepdims=False)
    small = (part * DOWN_X).astype(f16)
    small, freqs = lax.optimization_barrier((small, freqs))
    far, windows = 0.0, [block.astype(bf16)]
    for k, place_x in zip(NEAR, xs_near):
        piece = lax.dynamic_index_in_dim(small, place_x, 0, keepdims=False)
        piece = swap(jnp.concatenate([piece, block.astype(f16)], axis=0), "x", k)
        far = far + piece[: ys * rows].astype(f32)
        windows.append(piece[ys * rows :].astype(bf16))
    total = total + far * (1.0 / DOWN_X)

    freqs_far = swap(freqs, "c", 1)
    total, freqs_far = lax.optimization_barrier((total, freqs_far))
    ordered = []
    for i in range(ys):
        old = olds[0]
        for v, here in zip(olds[1:], from_near[i]):
            old = jnp.where(here, v, old)
        ordered.append(old)
    like = jax.ShapeDtypeStruct((rank, ys * rows), f32)
    lower, upper, inverse = on_vmem(
        gram_kernel,
        (jax.ShapeDtypeStruct((rank, rank), f32), like, like),
        freqs,
        freqs_far,
        *windows,
        jnp.concatenate(ordered, axis=0) * (1.0 / UP_U),
    )

    small = (total * DOWN_Y).astype(f16)
    p0, p2, p1, p3 = [small] + [swap(small, "y", k) for k in NEAR]
    mttkrp = (p1.astype(f32) + p3.astype(f32)) + (p0.astype(f32) + p2.astype(f32))
    updated, squares = on_vmem(
        sweep_kernel,
        (jax.ShapeDtypeStruct((ys * rows, rank), f32), jax.ShapeDtypeStruct((1, rank), f32)),
        mttkrp,
        lower,
        upper,
        inverse,
    )
    updated = lax.dynamic_slice_in_dim(updated, uy_rows, rows, 0)
    squares = squares + swap(squares, "c", 1)
    lines = xs * lax.axis_size("z")
    updated, squares = lax.optimization_barrier((updated, squares))
    squares = lax.all_to_all(
        jnp.broadcast_to(squares, (lines, rank)), ("z", "x"), 0, 0, tiled=True
    ).sum(axis=0)
    column_scale = jnp.sqrt(squares / (lines * 2 * ys * rows) + 1e-06)
    return (updated / column_scale[None, :], column_scale)


def solution(mesh):
    chan, win, freq = mesh.devices.shape
    fine = Mesh(mesh.devices.reshape(chan, win, freq // 2, 2), ("z", "x", "y", "c"))
    placed = (
        P("z", "x", ("y", "c")),
        P(("x", "y", "c"), None),
        P(("y", "c"), None),
        P(("z", "x", "y", "c"), None),
    )
    return jax.shard_map(
        body,
        mesh=fine,
        in_specs=placed,
        out_specs=(P(("z", "x", "y", "c"), None), P()),
        check_vma=False,
    )
```

```python
import jax
import jax.numpy as jnp
from jax import lax
from jax.experimental import pallas as pl
from jax.experimental.pallas import tpu as pltpu
from jax.sharding import Mesh, PartitionSpec as P

f32, bf16, f16 = jnp.float32, jnp.bfloat16, jnp.float16
DOWN_C, DOWN_X, DOWN_Y = 1.0 / 4, 1.0 / 8, 1.0 / 32
NEAR = (2, 1, 3)
LEAD = (1, 3, 2)
CHUNKS = 16


def on_vmem(kernel, outs, *args, scratch=()):
    place = pl.BlockSpec(memory_space=pltpu.VMEM)
    return pl.pallas_call(
        kernel,
        out_shape=outs,
        in_specs=[place] * len(args),
        out_specs=jax.tree.map(lambda _: place, outs),
        scratch_shapes=scratch,
        compiler_params=pltpu.CompilerParams(vmem_limit_bytes=32 * 2**20),
    )(*args)


def swap(value, axis, distance):
    count = lax.axis_size(axis)
    return lax.ppermute(value, axis, [(i, i ^ distance) for i in range(count)])


def flatten_kernel(spectrogram_ref, other_ref, mine_ref, buffer_ref, sem_ref):
    core = lax.axis_index("c")
    rows = spectrogram_ref.shape[0]
    chunk = other_ref.shape[0] // CHUNKS
    copies = []
    for side in range(2):
        for i in range(CHUNKS):
            offset = pl.multiple_of((2 * i + (core if side else 1 - core)) * chunk, chunk)
            copy = pltpu.make_async_copy(
                spectrogram_ref.at[pl.ds(offset, chunk)], buffer_ref.at[side, i], sem_ref.at[side, i]
            )
            copy.start()
            copies.append((side, i, copy))
    for side, i, copy in copies:
        copy.wait()
        out = mine_ref if side else other_ref
        out[chunk * i : chunk * (i + 1), :] = buffer_ref[side, i].reshape(chunk, out.shape[1])


def differ(part):
    lane = lax.broadcasted_iota(jnp.int32, part.shape, 1)
    return jnp.where(lane == 0, part, part - part[:, :1])


def other_kernel(flat_ref, block_ref, freq_ref, part_ref, khatri_rao_ref):
    freqs = freq_ref.shape[0]
    factor = freq_ref[...].astype(f32)
    for j in range(block_ref.shape[0]):
        khatri_rao_ref[freqs * j : freqs * (j + 1), :] = (block_ref[j : j + 1, :] * factor).astype(bf16)
    part_ref[...] = differ(jnp.dot(flat_ref[...], khatri_rao_ref[...], preferred_element_type=f32))


def mine_kernel(flat_ref, khatri_rao_ref, part_ref):
    part_ref[...] = differ(jnp.dot(flat_ref[...], khatri_rao_ref[...], preferred_element_type=f32))


def gram_of(block):
    return lax.dot_general(block, block, (((0,), (0,)), ((), ())), preferred_element_type=f32)


def gram_kernel(own_ref, far_ref, w0_ref, w2_ref, w1_ref, w3_ref, factor_ref, lower_ref, upper_ref, inverse_ref):
    rank = own_ref.shape[-1]

    def paired(own, one, three, two):
        return (gram_of(own) + gram_of(two)) + (gram_of(one) + gram_of(three))

    step = own_ref.shape[0] // 4
    freq = [paired(*[ref[step * i : step * (i + 1), :] for i in range(4)]) for ref in (own_ref, far_ref)]
    gram = (freq[0] + freq[1]) * paired(w0_ref[...], w1_ref[...], w3_ref[...], w2_ref[...])
    row = lax.broadcasted_iota(jnp.int32, (rank, rank), 0)
    col = lax.broadcasted_iota(jnp.int32, (rank, rank), 1)
    inverse = 1.0 / jnp.sum(jnp.where(row == col, gram, 0.0), axis=1, keepdims=True)
    lower_ref[...] = jnp.where(row > col, gram, 0.0) * inverse
    upper = jnp.where(row < col, gram, 0.0) * inverse
    upper_ref[...] = lax.dot_general(
        upper,
        factor_ref[...],
        (((1,), (1,)), ((), ())),
        precision=lax.Precision.HIGHEST,
        preferred_element_type=f32,
    )
    inverse_ref[...] = jnp.broadcast_to(inverse, inverse_ref.shape)


def sweep_kernel(mttkrp_ref, lower_ref, upper_ref, inverse_ref, out_ref, square_ref):
    coded = mttkrp_ref[...].T * (1.0 / DOWN_Y)
    rank, rows = coded.shape
    row = lax.broadcasted_iota(jnp.int32, (rank, rows), 0)
    mttkrp = jnp.where(row == 0, coded, coded + coded[:1, :])
    start = mttkrp * inverse_ref[...] - upper_ref[...]
    parts = [start[8 * i : 8 * i + 8] for i in range(rank // 8)]
    for j in range(rank):
        block, lane = divmod(j, 8)
        fresh = jnp.maximum(parts[block], 0.0)[lane : lane + 1, :]
        fresh = jnp.broadcast_to(fresh, (8, rows))
        for i in range(block, rank // 8):
            column = jnp.broadcast_to(lower_ref[8 * i : 8 * i + 8, j : j + 1], (8, rows))
            parts[i] = parts[i] - column * fresh
    updated = jnp.maximum(jnp.concatenate(parts, axis=0), 0.0).T
    out_ref[...] = updated
    square_ref[...] = jnp.sum(updated * updated, axis=0, keepdims=True)


def body(spectrogram, window_factor, freq_factor, channel_factor):
    chan_rows, win_rows, freq_rows = spectrogram.shape
    rows, rank = channel_factor.shape
    xs, ys = lax.axis_size("x"), lax.axis_size("y")
    x, y, c = lax.axis_index("x"), lax.axis_index("y"), lax.axis_index("c")
    ux, uy = x.astype(jnp.uint32), y.astype(jnp.uint32)
    xs_near = [ux ^ jnp.uint32(k) for k in NEAR]
    own_slots = [2 * (y ^ k) + c for k in (0,) + LEAD]
    far_slots = [2 * (y ^ k) + 1 - c for k in (0,) + LEAD]
    from_near = [[(y ^ i) == k for k in LEAD] for i in range(ys)]
    uy_rows = uy * jnp.uint32(rows)

    place = pl.BlockSpec(memory_space=pltpu.VMEM)
    high = channel_factor.astype(bf16)
    low = (channel_factor - high.astype(f32)).astype(bf16)
    first = jnp.concatenate([freq_factor, high, window_factor, low], axis=0)
    first, ux, xs_near, own_slots, far_slots, from_near, uy_rows = lax.optimization_barrier(
        (first, ux, xs_near, own_slots, far_slots, from_near, uy_rows)
    )
    first = [first] + [swap(first, "y", k) for k in LEAD]
    last = freq_rows + rows
    line = jnp.concatenate([v[last : last + 1] for v in first], axis=0)
    freqs = jnp.concatenate([v[:freq_rows] for v in first], axis=0)
    olds = [v[freq_rows:last].astype(f32) + v[last + 1 :].astype(f32) for v in first]
    width = win_rows * freq_rows
    half = jax.ShapeDtypeStruct((chan_rows // 2, width), bf16)
    place = pl.BlockSpec(memory_space=pltpu.VMEM)
    flat_other, flat_mine = pl.pallas_call(
        flatten_kernel,
        out_shape=(half, half),
        in_specs=[pl.BlockSpec(memory_space=pl.ANY)],
        out_specs=(place, place),
        scratch_shapes=[
            pltpu.VMEM((2, CHUNKS, rows, win_rows, freq_rows), bf16),
            pltpu.SemaphoreType.DMA((2, CHUNKS)),
        ],
        compiler_params=pltpu.CompilerParams(vmem_limit_bytes=48 * 2**20),
        cost_estimate=pl.CostEstimate(flops=0, bytes_accessed=chan_rows * width * 4, transcendentals=0),
    )(spectrogram)
    line, freqs, flat_other, flat_mine = lax.optimization_barrier((line, freqs, flat_other, flat_mine))
    pair = swap(line, "c", 1)
    slot = jnp.arange(win_rows)[:, None]
    block = jnp.zeros((win_rows, rank), f32)
    for i in range(ys):
        block = jnp.where(slot == own_slots[i], line[i : i + 1].astype(f32), block)
        block = jnp.where(slot == far_slots[i], pair[i : i + 1].astype(f32), block)
    half = jax.ShapeDtypeStruct((chan_rows // 2, rank), f32)
    other, khatri_rao = on_vmem(
        other_kernel, (half, jax.ShapeDtypeStruct((width, rank), bf16)), flat_other, block, freq_factor
    )
    mine = on_vmem(mine_kernel, half, flat_mine, khatri_rao)

    far = swap((other * DOWN_C).astype(f16), "c", 1).astype(f32)
    part = (mine + far * (1.0 / DOWN_C)).reshape(xs, ys * rows, rank)
    total = lax.dynamic_index_in_dim(part, ux, 0, keepdims=False)
    small = (part * DOWN_X).astype(f16)
    small, freqs = lax.optimization_barrier((small, freqs))
    pieces = [
        jnp.concatenate([lax.dynamic_index_in_dim(small, i, 0, keepdims=False), block.astype(f16)], axis=0)
        for i in xs_near
    ]
    pieces = [swap(v, "x", k) for v, k in zip(pieces, NEAR)]
    windows = [block.astype(bf16)] + [v[ys * rows :].astype(bf16) for v in pieces]
    two, one, three = (v[: ys * rows].astype(f32) for v in pieces)
    far = two + (one + three)
    total = total + far * (1.0 / DOWN_X)

    freqs_far = swap(freqs, "c", 1)
    total, freqs_far = lax.optimization_barrier((total, freqs_far))
    ordered = []
    for i in range(ys):
        old = olds[0]
        for v, here in zip(olds[1:], from_near[i]):
            old = jnp.where(here, v, old)
        ordered.append(old)
    like = jax.ShapeDtypeStruct((rank, ys * rows), f32)
    lower, upper, inverse = on_vmem(
        gram_kernel,
        (jax.ShapeDtypeStruct((rank, rank), f32), like, like),
        freqs,
        freqs_far,
        *windows,
        jnp.concatenate(ordered, axis=0),
    )

    small = (total * DOWN_Y).astype(f16)
    two, one, three = (v.astype(f32) for v in [swap(small, "y", k) for k in NEAR])
    mttkrp = (one + three) + (small.astype(f32) + two)
    updated, squares = on_vmem(
        sweep_kernel,
        (jax.ShapeDtypeStruct((ys * rows, rank), f32), jax.ShapeDtypeStruct((1, rank), f32)),
        mttkrp,
        lower,
        upper,
        inverse,
    )
    updated = lax.dynamic_slice_in_dim(updated, uy_rows, rows, 0)
    squares = squares + swap(squares, "c", 1)
    lines = xs * lax.axis_size("z")
    updated, squares = lax.optimization_barrier((updated, squares))
    order = [[(i + lines * 11 // 16) % lines for i in range(lines)]]
    squares = lax.all_to_all(
        jnp.broadcast_to(squares, (lines, rank)), ("z", "x"), 0, 0, tiled=True, axis_index_groups=order
    ).sum(axis=0)
    column_scale = jnp.sqrt(squares / (lines * 2 * ys * rows) + 1e-06)
    return (updated / column_scale[None, :], column_scale)


def solution(mesh):
    chan, win, freq = mesh.devices.shape
    fine = Mesh(mesh.devices.reshape(chan, win, freq // 2, 2), ("z", "x", "y", "c"))
    placed = (
        P("z", "x", ("y", "c")),
        P(("x", "y", "c"), None),
        P(("y", "c"), None),
        P(("z", "x", "y", "c"), None),
    )
    return jax.shard_map(
        body,
        mesh=fine,
        in_specs=placed,
        out_specs=(P(("z", "x", "y", "c"), None), P()),
        check_vma=False,
    )
```

```python
import jax
import jax.numpy as jnp
from jax import lax
from jax.experimental import pallas as pl
from jax.experimental.pallas import tpu as pltpu
from jax.sharding import Mesh, PartitionSpec as P

f32, bf16, f16 = jnp.float32, jnp.bfloat16, jnp.float16
DOWN_C, DOWN_X, DOWN_Y = 1.0 / 4, 1.0 / 8, 1.0 / 32
NEAR = (2, 1, 3)
LEAD = (1, 3, 2)
CHUNKS = 16


def on_vmem(kernel, outs, *args, scratch=()):
    place = pl.BlockSpec(memory_space=pltpu.VMEM)
    return pl.pallas_call(
        kernel,
        out_shape=outs,
        in_specs=[place] * len(args),
        out_specs=jax.tree.map(lambda _: place, outs),
        scratch_shapes=scratch,
        compiler_params=pltpu.CompilerParams(vmem_limit_bytes=32 * 2**20),
    )(*args)


def swap(value, axis, distance):
    count = lax.axis_size(axis)
    return lax.ppermute(value, axis, [(i, i ^ distance) for i in range(count)])


def flatten_kernel(spectrogram_ref, other_ref, mine_ref, buffer_ref, sem_ref):
    core = lax.axis_index("c")
    rows = spectrogram_ref.shape[0]
    chunk = other_ref.shape[0] // CHUNKS
    copies = []
    for side in range(2):
        for i in range(CHUNKS):
            offset = pl.multiple_of((2 * i + (core if side else 1 - core)) * chunk, chunk)
            copy = pltpu.make_async_copy(
                spectrogram_ref.at[pl.ds(offset, chunk)], buffer_ref.at[side, i], sem_ref.at[side, i]
            )
            copy.start()
            copies.append((side, i, copy))
    for side, i, copy in copies:
        copy.wait()
        out = mine_ref if side else other_ref
        out[chunk * i : chunk * (i + 1), :] = buffer_ref[side, i].reshape(chunk, out.shape[1])


def differ(part):
    lane = lax.broadcasted_iota(jnp.int32, part.shape, 1)
    return jnp.where(lane == 0, part, part - part[:, :1])


def other_kernel(flat_ref, block_ref, freq_ref, part_ref, khatri_rao_ref):
    freqs = freq_ref.shape[0]
    factor = freq_ref[...].astype(f32)
    for j in range(block_ref.shape[0]):
        khatri_rao_ref[freqs * j : freqs * (j + 1), :] = (block_ref[j : j + 1, :] * factor).astype(bf16)
    part_ref[...] = differ(jnp.dot(flat_ref[...], khatri_rao_ref[...], preferred_element_type=f32))


def mine_kernel(flat_ref, khatri_rao_ref, part_ref):
    part_ref[...] = differ(jnp.dot(flat_ref[...], khatri_rao_ref[...], preferred_element_type=f32))


def gram_of(block):
    return lax.dot_general(block, block, (((0,), (0,)), ((), ())), preferred_element_type=f32)


def gram_kernel(own_ref, far_ref, w0_ref, w2_ref, w1_ref, w3_ref, factor_ref, lower_ref, upper_ref, inverse_ref):
    rank = own_ref.shape[-1]

    def paired(own, one, three, two):
        return (gram_of(own) + gram_of(two)) + (gram_of(one) + gram_of(three))

    step = own_ref.shape[0] // 4
    freq = [paired(*[ref[step * i : step * (i + 1), :] for i in range(4)]) for ref in (own_ref, far_ref)]
    gram = (freq[0] + freq[1]) * paired(w0_ref[...], w1_ref[...], w3_ref[...], w2_ref[...])
    row = lax.broadcasted_iota(jnp.int32, (rank, rank), 0)
    col = lax.broadcasted_iota(jnp.int32, (rank, rank), 1)
    inverse = 1.0 / jnp.sum(jnp.where(row == col, gram, 0.0), axis=1, keepdims=True)
    lower_ref[...] = jnp.where(row > col, gram, 0.0) * inverse
    upper = jnp.where(row < col, gram, 0.0) * inverse
    upper_ref[...] = lax.dot_general(
        upper,
        factor_ref[...],
        (((1,), (1,)), ((), ())),
        precision=lax.Precision.HIGHEST,
        preferred_element_type=f32,
    )
    inverse_ref[...] = jnp.broadcast_to(inverse, inverse_ref.shape)


def sweep_kernel(mttkrp_ref, lower_ref, upper_ref, inverse_ref, out_ref, square_ref):
    coded = mttkrp_ref[...].T * (1.0 / DOWN_Y)
    rank, rows = coded.shape
    row = lax.broadcasted_iota(jnp.int32, (rank, rows), 0)
    mttkrp = jnp.where(row == 0, coded, coded + coded[:1, :])
    start = mttkrp * inverse_ref[...] - upper_ref[...]
    parts = [start[8 * i : 8 * i + 8] for i in range(rank // 8)]
    for j in range(rank):
        block, lane = divmod(j, 8)
        fresh = jnp.maximum(parts[block], 0.0)[lane : lane + 1, :]
        fresh = jnp.broadcast_to(fresh, (8, rows))
        for i in range(block, rank // 8):
            column = jnp.broadcast_to(lower_ref[8 * i : 8 * i + 8, j : j + 1], (8, rows))
            parts[i] = parts[i] - column * fresh
    updated = jnp.maximum(jnp.concatenate(parts, axis=0), 0.0).T
    out_ref[...] = updated
    square_ref[...] = jnp.sum(updated * updated, axis=0, keepdims=True)


def body(spectrogram, window_factor, freq_factor, channel_factor):
    chan_rows, win_rows, freq_rows = spectrogram.shape
    rows, rank = channel_factor.shape
    xs, ys = lax.axis_size("x"), lax.axis_size("y")
    x, y, c = lax.axis_index("x"), lax.axis_index("y"), lax.axis_index("c")
    ux, uy = x.astype(jnp.uint32), y.astype(jnp.uint32)
    xs_near = [ux ^ jnp.uint32(k) for k in NEAR]
    own_slots = [2 * (y ^ k) + c for k in (0,) + LEAD]
    far_slots = [2 * (y ^ k) + 1 - c for k in (0,) + LEAD]
    from_near = [[(y ^ i) == k for k in LEAD] for i in range(ys)]
    uy_rows = uy * jnp.uint32(rows)

    pair = swap(window_factor, "c", 1)
    high = channel_factor.astype(bf16)
    low = (channel_factor - high.astype(f32)).astype(bf16)
    base = jnp.concatenate([freq_factor, window_factor], axis=0)
    base, high, low = lax.optimization_barrier((base, high, low))
    first = jnp.concatenate([base, high, low, pair], axis=0)
    first, spectrogram, ux, xs_near, own_slots, far_slots, from_near, uy_rows = lax.optimization_barrier(
        (first, spectrogram, ux, xs_near, own_slots, far_slots, from_near, uy_rows)
    )
    first = [first] + [swap(first, "y", k) for k in LEAD]
    line = jnp.concatenate([v[freq_rows : freq_rows + 1] for v in first], axis=0)
    pair = jnp.concatenate([v[-1:] for v in first], axis=0)
    freqs = jnp.concatenate([v[:freq_rows] for v in first], axis=0)
    last = freq_rows + 1 + rows
    olds = [v[freq_rows + 1 : last].astype(f32) + v[last:-1].astype(f32) for v in first]
    width = win_rows * freq_rows
    half = jax.ShapeDtypeStruct((chan_rows // 2, width), bf16)
    place = pl.BlockSpec(memory_space=pltpu.VMEM)
    flat_other, flat_mine = pl.pallas_call(
        flatten_kernel,
        out_shape=(half, half),
        in_specs=[pl.BlockSpec(memory_space=pl.ANY)],
        out_specs=(place, place),
        scratch_shapes=[
            pltpu.VMEM((2, CHUNKS, rows, win_rows, freq_rows), bf16),
            pltpu.SemaphoreType.DMA((2, CHUNKS)),
        ],
        compiler_params=pltpu.CompilerParams(vmem_limit_bytes=48 * 2**20),
        cost_estimate=pl.CostEstimate(flops=0, bytes_accessed=chan_rows * width * 4, transcendentals=0),
    )(spectrogram)
    line, pair, freqs, flat_other, flat_mine = lax.optimization_barrier((line, pair, freqs, flat_other, flat_mine))
    slot = jnp.arange(win_rows)[:, None]
    block = jnp.zeros((win_rows, rank), f32)
    for i in range(ys):
        block = jnp.where(slot == own_slots[i], line[i : i + 1].astype(f32), block)
        block = jnp.where(slot == far_slots[i], pair[i : i + 1].astype(f32), block)
    half = jax.ShapeDtypeStruct((chan_rows // 2, rank), f32)
    other, khatri_rao = on_vmem(
        other_kernel, (half, jax.ShapeDtypeStruct((width, rank), bf16)), flat_other, block, freq_factor
    )
    mine = on_vmem(mine_kernel, half, flat_mine, khatri_rao)

    far = swap((other * DOWN_C).astype(f16), "c", 1).astype(f32)
    part = (mine + far * (1.0 / DOWN_C)).reshape(xs, ys * rows, rank)
    total = lax.dynamic_index_in_dim(part, ux, 0, keepdims=False)
    small = (part * DOWN_X).astype(f16)
    small, freqs = lax.optimization_barrier((small, freqs))
    pieces = [
        jnp.concatenate([lax.dynamic_index_in_dim(small, i, 0, keepdims=False), block.astype(f16)], axis=0)
        for i in xs_near
    ]
    pieces = [swap(v, "x", k) for v, k in zip(pieces, NEAR)]
    windows = [block.astype(bf16)] + [v[ys * rows :].astype(bf16) for v in pieces]
    two, one, three = (v[: ys * rows].astype(f32) for v in pieces)
    far = two + (one + three)
    total = total + far * (1.0 / DOWN_X)

    freqs_far = swap(freqs, "c", 1)
    total, freqs_far = lax.optimization_barrier((total, freqs_far))
    ordered = []
    for i in range(ys):
        old = olds[0]
        for v, here in zip(olds[1:], from_near[i]):
            old = jnp.where(here, v, old)
        ordered.append(old)
    like = jax.ShapeDtypeStruct((rank, ys * rows), f32)
    lower, upper, inverse = on_vmem(
        gram_kernel,
        (jax.ShapeDtypeStruct((rank, rank), f32), like, like),
        freqs,
        freqs_far,
        *windows,
        jnp.concatenate(ordered, axis=0),
    )

    small = (total * DOWN_Y).astype(f16)
    two, one, three = (v.astype(f32) for v in [swap(small, "y", k) for k in NEAR])
    mttkrp = (one + three) + (small.astype(f32) + two)
    updated, squares = on_vmem(
        sweep_kernel,
        (jax.ShapeDtypeStruct((ys * rows, rank), f32), jax.ShapeDtypeStruct((1, rank), f32)),
        mttkrp,
        lower,
        upper,
        inverse,
    )
    updated = lax.dynamic_slice_in_dim(updated, uy_rows, rows, 0)
    squares = squares + swap(squares, "c", 1)
    lines = xs * lax.axis_size("z")
    updated, squares = lax.optimization_barrier((updated, squares))
    order = [[(i + lines * 11 // 16) % lines for i in range(lines)]]
    squares = lax.all_to_all(
        jnp.broadcast_to(squares, (lines, rank)), ("z", "x"), 0, 0, tiled=True, axis_index_groups=order
    ).sum(axis=0)
    column_scale = jnp.sqrt(squares / (lines * 2 * ys * rows) + 1e-06)
    return (updated / column_scale[None, :], column_scale)


def solution(mesh):
    chan, win, freq = mesh.devices.shape
    fine = Mesh(mesh.devices.reshape(chan, win, freq // 2, 2), ("z", "x", "y", "c"))
    placed = (
        P("z", "x", ("y", "c")),
        P(("x", "y", "c"), None),
        P(("y", "c"), None),
        P(("z", "x", "y", "c"), None),
    )
    return jax.shard_map(
        body,
        mesh=fine,
        in_specs=placed,
        out_specs=(P(("z", "x", "y", "c"), None), P()),
        check_vma=False,
    )
```

```python
import jax
import jax.numpy as jnp
from jax import lax
from jax.experimental import pallas as pl
from jax.experimental.pallas import tpu as pltpu
from jax.sharding import Mesh, PartitionSpec as P

f32, bf16, f16 = jnp.float32, jnp.bfloat16, jnp.float16
DOWN_C, DOWN_X, DOWN_Y = 1.0 / 4, 1.0 / 8, 1.0 / 32
UP_U = 1024.0
NEAR = (2, 1, 3)
LEAD = (1, 3, 2)
CHUNKS = 16


def on_vmem(kernel, outs, *args, scratch=()):
    place = pl.BlockSpec(memory_space=pltpu.VMEM)
    return pl.pallas_call(
        kernel,
        out_shape=outs,
        in_specs=[place] * len(args),
        out_specs=jax.tree.map(lambda _: place, outs),
        scratch_shapes=scratch,
        compiler_params=pltpu.CompilerParams(vmem_limit_bytes=32 * 2**20),
    )(*args)


def swap(value, axis, distance):
    count = lax.axis_size(axis)
    return lax.ppermute(value, axis, [(i, i ^ distance) for i in range(count)])


def flatten_kernel(spectrogram_ref, other_ref, mine_ref, buffer_ref, sem_ref):
    core = lax.axis_index("c")
    rows = spectrogram_ref.shape[0]
    chunk = other_ref.shape[0] // CHUNKS
    copies = []
    for side in range(2):
        for i in range(CHUNKS):
            offset = pl.multiple_of((2 * i + (core if side else 1 - core)) * chunk, chunk)
            copy = pltpu.make_async_copy(
                spectrogram_ref.at[pl.ds(offset, chunk)], buffer_ref.at[side, i], sem_ref.at[side, i]
            )
            copy.start()
            copies.append((side, i, copy))
    for side, i, copy in copies:
        copy.wait()
        out = mine_ref if side else other_ref
        out[chunk * i : chunk * (i + 1), :] = buffer_ref[side, i].reshape(chunk, out.shape[1])


def scale_kernel(factor_ref, out_ref):
    out_ref[...] = factor_ref[...] * UP_U


def differ(part):
    lane = lax.broadcasted_iota(jnp.int32, part.shape, 1)
    return jnp.where(lane == 0, part, part - part[:, :1])


def other_kernel(flat_ref, block_ref, freq_ref, part_ref, khatri_rao_ref):
    freqs = freq_ref.shape[0]
    factor = freq_ref[...].astype(f32)
    for j in range(block_ref.shape[0]):
        khatri_rao_ref[freqs * j : freqs * (j + 1), :] = (block_ref[j : j + 1, :] * factor).astype(bf16)
    part_ref[...] = differ(jnp.dot(flat_ref[...], khatri_rao_ref[...], preferred_element_type=f32))


def mine_kernel(flat_ref, khatri_rao_ref, part_ref):
    part_ref[...] = differ(jnp.dot(flat_ref[...], khatri_rao_ref[...], preferred_element_type=f32))


def gram_of(block):
    return lax.dot_general(block, block, (((0,), (0,)), ((), ())), preferred_element_type=f32)


def gram_kernel(own_ref, far_ref, w0_ref, w2_ref, w1_ref, w3_ref, factor_ref, lower_ref, upper_ref, inverse_ref):
    rank = own_ref.shape[-1]

    def paired(own, one, three, two):
        return (gram_of(own) + gram_of(two)) + (gram_of(one) + gram_of(three))

    step = own_ref.shape[0] // 4
    freq = [paired(*[ref[step * i : step * (i + 1), :] for i in range(4)]) for ref in (own_ref, far_ref)]
    gram = (freq[0] + freq[1]) * paired(w0_ref[...], w1_ref[...], w3_ref[...], w2_ref[...])
    row = lax.broadcasted_iota(jnp.int32, (rank, rank), 0)
    col = lax.broadcasted_iota(jnp.int32, (rank, rank), 1)
    inverse = 1.0 / jnp.sum(jnp.where(row == col, gram, 0.0), axis=1, keepdims=True)
    lower_ref[...] = jnp.where(row > col, gram, 0.0) * inverse
    upper = jnp.where(row < col, gram, 0.0) * inverse
    upper_ref[...] = lax.dot_general(
        upper,
        factor_ref[...],
        (((1,), (1,)), ((), ())),
        precision=lax.Precision.HIGHEST,
        preferred_element_type=f32,
    )
    inverse_ref[...] = jnp.broadcast_to(inverse, inverse_ref.shape)


def sweep_kernel(mttkrp_ref, lower_ref, upper_ref, inverse_ref, out_ref, square_ref):
    coded = mttkrp_ref[...].T * (1.0 / DOWN_Y)
    rank, rows = coded.shape
    row = lax.broadcasted_iota(jnp.int32, (rank, rows), 0)
    mttkrp = jnp.where(row == 0, coded, coded + coded[:1, :])
    start = mttkrp * inverse_ref[...] - upper_ref[...]
    parts = [start[8 * i : 8 * i + 8] for i in range(rank // 8)]
    for j in range(rank):
        block, lane = divmod(j, 8)
        fresh = jnp.maximum(parts[block], 0.0)[lane : lane + 1, :]
        fresh = jnp.broadcast_to(fresh, (8, rows))
        for i in range(block, rank // 8):
            column = jnp.broadcast_to(lower_ref[8 * i : 8 * i + 8, j : j + 1], (8, rows))
            parts[i] = parts[i] - column * fresh
    updated = jnp.maximum(jnp.concatenate(parts, axis=0), 0.0).T
    out_ref[...] = updated
    square_ref[...] = jnp.sum(updated * updated, axis=0, keepdims=True)


def body(spectrogram, window_factor, freq_factor, channel_factor):
    chan_rows, win_rows, freq_rows = spectrogram.shape
    rows, rank = channel_factor.shape
    xs, ys = lax.axis_size("x"), lax.axis_size("y")
    x, y, c = lax.axis_index("x"), lax.axis_index("y"), lax.axis_index("c")
    ux, uy = x.astype(jnp.uint32), y.astype(jnp.uint32)
    xs_near = [ux ^ jnp.uint32(k) for k in NEAR]
    own_slots = [2 * (y ^ k) + c for k in (0,) + LEAD]
    far_slots = [2 * (y ^ k) + 1 - c for k in (0,) + LEAD]
    from_near = [[(y ^ i) == k for k in LEAD] for i in range(ys)]
    uy_rows = uy * jnp.uint32(rows)

    pair = swap(window_factor, "c", 1)
    base = jnp.concatenate([freq_factor, window_factor], axis=0)
    base, factor = lax.optimization_barrier((base, channel_factor))
    scaled = on_vmem(scale_kernel, jax.ShapeDtypeStruct(factor.shape, f32), factor).astype(f16)
    first = jnp.concatenate([base.astype(f16), scaled, pair.astype(f16)], axis=0)
    first, spectrogram, ux, xs_near, own_slots, far_slots, from_near, uy_rows = lax.optimization_barrier(
        (first, spectrogram, ux, xs_near, own_slots, far_slots, from_near, uy_rows)
    )
    first = [first] + [swap(first, "y", k) for k in LEAD]
    line = jnp.concatenate([v[freq_rows : freq_rows + 1] for v in first], axis=0)
    pair = jnp.concatenate([v[-1:] for v in first], axis=0)
    freqs = jnp.concatenate([v[:freq_rows] for v in first], axis=0).astype(bf16)
    olds = [v[freq_rows + 1 : -1].astype(f32) for v in first]
    width = win_rows * freq_rows
    half = jax.ShapeDtypeStruct((chan_rows // 2, width), bf16)
    place = pl.BlockSpec(memory_space=pltpu.VMEM)
    flat_other, flat_mine = pl.pallas_call(
        flatten_kernel,
        out_shape=(half, half),
        in_specs=[pl.BlockSpec(memory_space=pl.ANY)],
        out_specs=(place, place),
        scratch_shapes=[
            pltpu.VMEM((2, CHUNKS, rows, win_rows, freq_rows), bf16),
            pltpu.SemaphoreType.DMA((2, CHUNKS)),
        ],
        compiler_params=pltpu.CompilerParams(vmem_limit_bytes=48 * 2**20),
        cost_estimate=pl.CostEstimate(flops=0, bytes_accessed=chan_rows * width * 4, transcendentals=0),
    )(spectrogram)
    line, pair, flat_other, flat_mine = lax.optimization_barrier((line, pair, flat_other, flat_mine))
    slot = jnp.arange(win_rows)[:, None]
    block = jnp.zeros((win_rows, rank), f32)
    for i in range(ys):
        block = jnp.where(slot == own_slots[i], line[i : i + 1].astype(f32), block)
        block = jnp.where(slot == far_slots[i], pair[i : i + 1].astype(f32), block)
    half = jax.ShapeDtypeStruct((chan_rows // 2, rank), f32)
    other, khatri_rao = on_vmem(
        other_kernel, (half, jax.ShapeDtypeStruct((width, rank), bf16)), flat_other, block, freq_factor
    )
    mine = on_vmem(mine_kernel, half, flat_mine, khatri_rao)

    far = swap((other * DOWN_C).astype(f16), "c", 1).astype(f32)
    part = (mine + far * (1.0 / DOWN_C)).reshape(xs, ys * rows, rank)
    total = lax.dynamic_index_in_dim(part, ux, 0, keepdims=False)
    small = (part * DOWN_X).astype(f16)
    small, freqs = lax.optimization_barrier((small, freqs))
    pieces = [
        jnp.concatenate([lax.dynamic_index_in_dim(small, i, 0, keepdims=False), block.astype(f16)], axis=0)
        for i in xs_near
    ]
    pieces = [swap(v, "x", k) for v, k in zip(pieces, NEAR)]
    windows = [block.astype(bf16)] + [v[ys * rows :].astype(bf16) for v in pieces]
    two, one, three = (v[: ys * rows].astype(f32) for v in pieces)
    far = two + (one + three)
    total = total + far * (1.0 / DOWN_X)

    freqs_far = swap(freqs, "c", 1)
    total, freqs_far = lax.optimization_barrier((total, freqs_far))
    ordered = []
    for i in range(ys):
        old = olds[0]
        for v, here in zip(olds[1:], from_near[i]):
            old = jnp.where(here, v, old)
        ordered.append(old)
    like = jax.ShapeDtypeStruct((rank, ys * rows), f32)
    lower, upper, inverse = on_vmem(
        gram_kernel,
        (jax.ShapeDtypeStruct((rank, rank), f32), like, like),
        freqs,
        freqs_far,
        *windows,
        jnp.concatenate(ordered, axis=0) * (1.0 / UP_U),
    )

    small = (total * DOWN_Y).astype(f16)
    two, one, three = (v.astype(f32) for v in [swap(small, "y", k) for k in NEAR])
    mttkrp = (one + three) + (small.astype(f32) + two)
    updated, squares = on_vmem(
        sweep_kernel,
        (jax.ShapeDtypeStruct((ys * rows, rank), f32), jax.ShapeDtypeStruct((1, rank), f32)),
        mttkrp,
        lower,
        upper,
        inverse,
    )
    updated = lax.dynamic_slice_in_dim(updated, uy_rows, rows, 0)
    squares = squares + swap(squares, "c", 1)
    lines = xs * lax.axis_size("z")
    updated, squares = lax.optimization_barrier((updated, squares))
    order = [[(i + lines * 11 // 16) % lines for i in range(lines)]]
    squares = lax.all_to_all(
        jnp.broadcast_to(squares, (lines, rank)), ("z", "x"), 0, 0, tiled=True, axis_index_groups=order
    ).sum(axis=0)
    column_scale = jnp.sqrt(squares / (lines * 2 * ys * rows) + 1e-06)
    return (updated / column_scale[None, :], column_scale)


def solution(mesh):
    chan, win, freq = mesh.devices.shape
    fine = Mesh(mesh.devices.reshape(chan, win, freq // 2, 2), ("z", "x", "y", "c"))
    placed = (
        P("z", "x", ("y", "c")),
        P(("x", "y", "c"), None),
        P(("y", "c"), None),
        P(("z", "x", "y", "c"), None),
    )
    return jax.shard_map(
        body,
        mesh=fine,
        in_specs=placed,
        out_specs=(P(("z", "x", "y", "c"), None), P()),
        check_vma=False,
    )
```

```python
import jax
import jax.numpy as jnp
from jax import lax
from jax.experimental import pallas as pl
from jax.experimental.pallas import tpu as pltpu
from jax.sharding import Mesh, PartitionSpec as P

f32, bf16, f16 = jnp.float32, jnp.bfloat16, jnp.float16
DOWN_C, DOWN_X, DOWN_Y = 1.0 / 4, 1.0 / 8, 1.0 / 32
UP_U = 1024.0
NEAR = (2, 1, 3)
LEAD = (1, 3, 2)
CHUNKS = 16


def on_vmem(kernel, outs, *args, scratch=()):
    place = pl.BlockSpec(memory_space=pltpu.VMEM)
    return pl.pallas_call(
        kernel,
        out_shape=outs,
        in_specs=[place] * len(args),
        out_specs=jax.tree.map(lambda _: place, outs),
        scratch_shapes=scratch,
        compiler_params=pltpu.CompilerParams(vmem_limit_bytes=32 * 2**20),
    )(*args)


def swap(value, axis, distance):
    count = lax.axis_size(axis)
    return lax.ppermute(value, axis, [(i, i ^ distance) for i in range(count)])


def flatten_kernel(spectrogram_ref, other_ref, mine_ref, buffer_ref, sem_ref):
    core = lax.axis_index("c")
    rows = spectrogram_ref.shape[0]
    chunk = other_ref.shape[0] // CHUNKS
    copies = []
    for side in range(2):
        for i in range(CHUNKS):
            offset = pl.multiple_of((2 * i + (core if side else 1 - core)) * chunk, chunk)
            copy = pltpu.make_async_copy(
                spectrogram_ref.at[pl.ds(offset, chunk)], buffer_ref.at[side, i], sem_ref.at[side, i]
            )
            copy.start()
            copies.append((side, i, copy))
    for side, i, copy in copies:
        copy.wait()
        out = mine_ref if side else other_ref
        out[chunk * i : chunk * (i + 1), :] = buffer_ref[side, i].reshape(chunk, out.shape[1])


def scale_kernel(factor_ref, out_ref):
    out_ref[...] = factor_ref[...] * UP_U


def differ(part):
    lane = lax.broadcasted_iota(jnp.int32, part.shape, 1)
    return jnp.where(lane == 0, part, part - part[:, :1])


def other_kernel(flat_ref, block_ref, freq_ref, part_ref, khatri_rao_ref):
    freqs = freq_ref.shape[0]
    factor = freq_ref[...].astype(f32)
    for j in range(block_ref.shape[0]):
        khatri_rao_ref[freqs * j : freqs * (j + 1), :] = (block_ref[j : j + 1, :] * factor).astype(bf16)
    part_ref[...] = differ(jnp.dot(flat_ref[...], khatri_rao_ref[...], preferred_element_type=f32))


def mine_kernel(flat_ref, khatri_rao_ref, part_ref):
    part_ref[...] = differ(jnp.dot(flat_ref[...], khatri_rao_ref[...], preferred_element_type=f32))


def gram_of(block):
    return lax.dot_general(block, block, (((0,), (0,)), ((), ())), preferred_element_type=f32)


def gram_kernel(own_ref, far_ref, w0_ref, w2_ref, w1_ref, w3_ref, factor_ref, spread_ref, upper_ref, inverse_ref):
    rank = own_ref.shape[-1]

    def paired(own, one, three, two):
        return (gram_of(own) + gram_of(two)) + (gram_of(one) + gram_of(three))

    step = own_ref.shape[0] // 4
    freq = [paired(*[ref[step * i : step * (i + 1), :] for i in range(4)]) for ref in (own_ref, far_ref)]
    gram = (freq[0] + freq[1]) * paired(w0_ref[...], w1_ref[...], w3_ref[...], w2_ref[...])
    row = lax.broadcasted_iota(jnp.int32, (rank, rank), 0)
    col = lax.broadcasted_iota(jnp.int32, (rank, rank), 1)
    inverse = 1.0 / jnp.sum(jnp.where(row == col, gram, 0.0), axis=1, keepdims=True)
    lower = jnp.where(row > col, gram, 0.0) * inverse
    for j in range(rank):
        block = j // 8 * 8
        spread_ref[j, block:, :] = jnp.broadcast_to(lower[block:, j : j + 1], (rank - block, rank))
    upper = jnp.where(row < col, gram, 0.0) * inverse
    upper_ref[...] = lax.dot_general(
        upper,
        factor_ref[...],
        (((1,), (1,)), ((), ())),
        precision=lax.Precision.HIGHEST,
        preferred_element_type=f32,
    )
    inverse_ref[...] = jnp.broadcast_to(inverse, inverse_ref.shape)


def sweep_kernel(mttkrp_ref, spread_ref, upper_ref, inverse_ref, out_ref, square_ref):
    coded = mttkrp_ref[...].T * (1.0 / DOWN_Y)
    rank, rows = coded.shape
    row = lax.broadcasted_iota(jnp.int32, (rank, rows), 0)
    mttkrp = jnp.where(row == 0, coded, coded + coded[:1, :])
    start = mttkrp * inverse_ref[...] - upper_ref[...]
    groups = range(rows // rank)
    parts = [[start[8 * i : 8 * i + 8, rank * g : rank * (g + 1)] for g in groups] for i in range(rank // 8)]
    for j in range(rank):
        block, lane = divmod(j, 8)
        fresh = [
            jnp.broadcast_to(jnp.maximum(parts[block][g], 0.0)[lane : lane + 1, :], (8, rank)) for g in groups
        ]
        for i in range(block, rank // 8):
            column = spread_ref[j, 8 * i : 8 * i + 8, :]
            for g in groups:
                parts[i][g] = parts[i][g] - column * fresh[g]
    final = jnp.concatenate([jnp.concatenate(p, axis=1) for p in parts], axis=0)
    updated = jnp.maximum(final, 0.0).T
    out_ref[...] = updated
    square_ref[...] = jnp.sum(updated * updated, axis=0, keepdims=True)


def body(spectrogram, window_factor, freq_factor, channel_factor):
    chan_rows, win_rows, freq_rows = spectrogram.shape
    rows, rank = channel_factor.shape
    xs, ys = lax.axis_size("x"), lax.axis_size("y")
    x, y, c = lax.axis_index("x"), lax.axis_index("y"), lax.axis_index("c")
    ux, uy = x.astype(jnp.uint32), y.astype(jnp.uint32)
    xs_near = [ux ^ jnp.uint32(k) for k in NEAR]
    own_slots = [2 * (y ^ k) + c for k in (0,) + LEAD]
    far_slots = [2 * (y ^ k) + 1 - c for k in (0,) + LEAD]
    from_near = [[(y ^ i) == k for k in LEAD] for i in range(ys)]
    uy_rows = uy * jnp.uint32(rows)

    pair = swap(window_factor, "c", 1)
    base = jnp.concatenate([freq_factor, window_factor], axis=0)
    base, factor = lax.optimization_barrier((base, channel_factor))
    scaled = on_vmem(scale_kernel, jax.ShapeDtypeStruct(factor.shape, f32), factor).astype(f16)
    first = jnp.concatenate([base.astype(f16), scaled, pair.astype(f16)], axis=0)
    first, spectrogram, ux, xs_near, own_slots, far_slots, from_near, uy_rows = lax.optimization_barrier(
        (first, spectrogram, ux, xs_near, own_slots, far_slots, from_near, uy_rows)
    )
    first = [first] + [swap(first, "y", k) for k in LEAD]
    line = jnp.concatenate([v[freq_rows : freq_rows + 1] for v in first], axis=0)
    pair = jnp.concatenate([v[-1:] for v in first], axis=0)
    freqs = jnp.concatenate([v[:freq_rows] for v in first], axis=0).astype(bf16)
    olds = [v[freq_rows + 1 : -1].astype(f32) for v in first]
    width = win_rows * freq_rows
    half = jax.ShapeDtypeStruct((chan_rows // 2, width), bf16)
    place = pl.BlockSpec(memory_space=pltpu.VMEM)
    flat_other, flat_mine = pl.pallas_call(
        flatten_kernel,
        out_shape=(half, half),
        in_specs=[pl.BlockSpec(memory_space=pl.ANY)],
        out_specs=(place, place),
        scratch_shapes=[
            pltpu.VMEM((2, CHUNKS, rows, win_rows, freq_rows), bf16),
            pltpu.SemaphoreType.DMA((2, CHUNKS)),
        ],
        compiler_params=pltpu.CompilerParams(vmem_limit_bytes=48 * 2**20),
        cost_estimate=pl.CostEstimate(flops=0, bytes_accessed=chan_rows * width * 4, transcendentals=0),
    )(spectrogram)
    line, pair, flat_other, flat_mine = lax.optimization_barrier((line, pair, flat_other, flat_mine))
    slot = jnp.arange(win_rows)[:, None]
    block = jnp.zeros((win_rows, rank), f32)
    for i in range(ys):
        block = jnp.where(slot == own_slots[i], line[i : i + 1].astype(f32), block)
        block = jnp.where(slot == far_slots[i], pair[i : i + 1].astype(f32), block)
    half = jax.ShapeDtypeStruct((chan_rows // 2, rank), f32)
    other, khatri_rao = on_vmem(
        other_kernel, (half, jax.ShapeDtypeStruct((width, rank), bf16)), flat_other, block, freq_factor
    )
    mine = on_vmem(mine_kernel, half, flat_mine, khatri_rao)

    far = swap((other * DOWN_C).astype(f16), "c", 1).astype(f32)
    part = (mine + far * (1.0 / DOWN_C)).reshape(xs, ys * rows, rank)
    total = lax.dynamic_index_in_dim(part, ux, 0, keepdims=False)
    small = (part * DOWN_X).astype(f16)
    small, freqs = lax.optimization_barrier((small, freqs))
    pieces = [
        jnp.concatenate([lax.dynamic_index_in_dim(small, i, 0, keepdims=False), block.astype(f16)], axis=0)
        for i in xs_near
    ]
    pieces = [swap(v, "x", k) for v, k in zip(pieces, NEAR)]
    windows = [block.astype(bf16)] + [v[ys * rows :].astype(bf16) for v in pieces]
    two, one, three = (v[: ys * rows].astype(f32) for v in pieces)
    far = two + (one + three)
    total = total + far * (1.0 / DOWN_X)

    freqs_far = swap(freqs, "c", 1)
    total, freqs_far = lax.optimization_barrier((total, freqs_far))
    ordered = []
    for i in range(ys):
        old = olds[0]
        for v, here in zip(olds[1:], from_near[i]):
            old = jnp.where(here, v, old)
        ordered.append(old)
    like = jax.ShapeDtypeStruct((rank, ys * rows), f32)
    spread, upper, inverse = on_vmem(
        gram_kernel,
        (jax.ShapeDtypeStruct((rank, rank, rank), f32), like, like),
        freqs,
        freqs_far,
        *windows,
        jnp.concatenate(ordered, axis=0) * (1.0 / UP_U),
    )

    small = (total * DOWN_Y).astype(f16)
    two, one, three = (v.astype(f32) for v in [swap(small, "y", k) for k in NEAR])
    mttkrp = (one + three) + (small.astype(f32) + two)
    updated, squares = on_vmem(
        sweep_kernel,
        (jax.ShapeDtypeStruct((ys * rows, rank), f32), jax.ShapeDtypeStruct((1, rank), f32)),
        mttkrp,
        spread,
        upper,
        inverse,
    )
    updated = lax.dynamic_slice_in_dim(updated, uy_rows, rows, 0)
    squares = squares + swap(squares, "c", 1)
    lines = xs * lax.axis_size("z")
    updated, squares = lax.optimization_barrier((updated, squares))
    order = [[(i + lines * 11 // 16) % lines for i in range(lines)]]
    squares = lax.all_to_all(
        jnp.broadcast_to(squares, (lines, rank)), ("z", "x"), 0, 0, tiled=True, axis_index_groups=order
    ).sum(axis=0)
    column_scale = jnp.sqrt(squares / (lines * 2 * ys * rows) + 1e-06)
    return (updated / column_scale[None, :], column_scale)


def solution(mesh):
    chan, win, freq = mesh.devices.shape
    fine = Mesh(mesh.devices.reshape(chan, win, freq // 2, 2), ("z", "x", "y", "c"))
    placed = (
        P("z", "x", ("y", "c")),
        P(("x", "y", "c"), None),
        P(("y", "c"), None),
        P(("z", "x", "y", "c"), None),
    )
    return jax.shard_map(
        body,
        mesh=fine,
        in_specs=placed,
        out_specs=(P(("z", "x", "y", "c"), None), P()),
        check_vma=False,
    )
```

```python
import jax
import jax.numpy as jnp
from jax import lax
from jax.experimental import pallas as pl
from jax.experimental.pallas import tpu as pltpu
from jax.sharding import Mesh, PartitionSpec as P

f32, bf16, f16 = jnp.float32, jnp.bfloat16, jnp.float16
DOWN_C, DOWN_X, DOWN_Y = 1.0 / 4, 1.0 / 8, 1.0 / 32
UP_U = 1024.0
NEAR = (2, 1, 3)
LEAD = (1, 3, 2)
CHUNKS = 16


def on_vmem(kernel, outs, *args, scratch=()):
    place = pl.BlockSpec(memory_space=pltpu.VMEM)
    return pl.pallas_call(
        kernel,
        out_shape=outs,
        in_specs=[place] * len(args),
        out_specs=jax.tree.map(lambda _: place, outs),
        scratch_shapes=scratch,
        compiler_params=pltpu.CompilerParams(vmem_limit_bytes=32 * 2**20),
    )(*args)


def swap(value, axis, distance):
    count = lax.axis_size(axis)
    return lax.ppermute(value, axis, [(i, i ^ distance) for i in range(count)])


def flatten_kernel(spectrogram_ref, other_ref, mine_ref, buffer_ref, sem_ref):
    core = lax.axis_index("c")
    rows = spectrogram_ref.shape[0]
    chunk = other_ref.shape[0] // CHUNKS
    copies = []
    for side in range(2):
        for i in range(CHUNKS):
            offset = pl.multiple_of((2 * i + (core if side else 1 - core)) * chunk, chunk)
            copy = pltpu.make_async_copy(
                spectrogram_ref.at[pl.ds(offset, chunk)], buffer_ref.at[side, i], sem_ref.at[side, i]
            )
            copy.start()
            copies.append((side, i, copy))
    for side, i, copy in copies:
        copy.wait()
        out = mine_ref if side else other_ref
        out[chunk * i : chunk * (i + 1), :] = buffer_ref[side, i].reshape(chunk, out.shape[1])


def scale_kernel(factor_ref, out_ref):
    out_ref[...] = factor_ref[...] * UP_U


def differ(part):
    lane = lax.broadcasted_iota(jnp.int32, part.shape, 1)
    return jnp.where(lane == 0, part, part - part[:, :1])


def other_kernel(flat_ref, block_ref, freq_ref, part_ref, khatri_rao_ref):
    freqs = freq_ref.shape[0]
    factor = freq_ref[...].astype(f32)
    for j in range(block_ref.shape[0]):
        khatri_rao_ref[freqs * j : freqs * (j + 1), :] = (block_ref[j : j + 1, :] * factor).astype(bf16)
    part_ref[...] = differ(jnp.dot(flat_ref[...], khatri_rao_ref[...], preferred_element_type=f32))


def mine_kernel(flat_ref, khatri_rao_ref, part_ref):
    part_ref[...] = differ(jnp.dot(flat_ref[...], khatri_rao_ref[...], preferred_element_type=f32))


def gram_of(block):
    return lax.dot_general(block, block, (((0,), (0,)), ((), ())), preferred_element_type=f32)


def gram_kernel(own_ref, far_ref, w0_ref, w2_ref, w1_ref, w3_ref, factor_ref, spread_ref, upper_ref, inverse_ref):
    rank = own_ref.shape[-1]

    def paired(own, one, three, two):
        return (gram_of(own) + gram_of(two)) + (gram_of(one) + gram_of(three))

    step = own_ref.shape[0] // 4
    freq = [paired(*[ref[step * i : step * (i + 1), :] for i in range(4)]) for ref in (own_ref, far_ref)]
    gram = (freq[0] + freq[1]) * paired(w0_ref[...], w1_ref[...], w3_ref[...], w2_ref[...])
    row = lax.broadcasted_iota(jnp.int32, (rank, rank), 0)
    col = lax.broadcasted_iota(jnp.int32, (rank, rank), 1)
    inverse = 1.0 / jnp.sum(jnp.where(row == col, gram, 0.0), axis=1, keepdims=True)
    lower = jnp.where(row > col, gram, 0.0) * inverse
    for j in range(rank):
        block = j // 8 * 8
        spread_ref[j, block:, :] = jnp.broadcast_to(lower[block:, j : j + 1], (rank - block, rank))
    upper = jnp.where(row < col, gram, 0.0) * inverse
    upper_ref[...] = lax.dot_general(
        upper,
        factor_ref[...],
        (((1,), (1,)), ((), ())),
        precision=lax.Precision.HIGHEST,
        preferred_element_type=f32,
    )
    inverse_ref[...] = jnp.broadcast_to(inverse, inverse_ref.shape)


def sweep_kernel(mttkrp_ref, spread_ref, upper_ref, inverse_ref, out_ref, square_ref):
    coded = mttkrp_ref[...].T * (1.0 / DOWN_Y)
    rank, rows = coded.shape
    row = lax.broadcasted_iota(jnp.int32, (rank, rows), 0)
    mttkrp = jnp.where(row == 0, coded, coded + coded[:1, :])
    start = mttkrp * inverse_ref[...] - upper_ref[...]
    groups = range(rows // rank)
    parts = [[start[8 * i : 8 * i + 8, rank * g : rank * (g + 1)] for g in groups] for i in range(rank // 8)]
    for j in range(rank):
        block, lane = divmod(j, 8)
        fresh = [
            jnp.broadcast_to(jnp.maximum(parts[block][g], 0.0)[lane : lane + 1, :], (8, rank)) for g in groups
        ]
        for i in range(block, rank // 8):
            column = spread_ref[j, 8 * i : 8 * i + 8, :]
            for g in groups:
                parts[i][g] = parts[i][g] - column * fresh[g]
    final = jnp.concatenate([jnp.concatenate(p, axis=1) for p in parts], axis=0)
    updated = jnp.maximum(final, 0.0).T
    out_ref[...] = updated
    square_ref[...] = jnp.sum(updated * updated, axis=0, keepdims=True)


def body(spectrogram, window_factor, freq_factor, channel_factor):
    chan_rows, win_rows, freq_rows = spectrogram.shape
    rows, rank = channel_factor.shape
    xs, ys = lax.axis_size("x"), lax.axis_size("y")
    x, y, c = lax.axis_index("x"), lax.axis_index("y"), lax.axis_index("c")
    ux, uy = x.astype(jnp.uint32), y.astype(jnp.uint32)
    xs_near = [ux ^ jnp.uint32(k) for k in NEAR]
    own_slots = [2 * (y ^ k) + c for k in (0,) + LEAD]
    far_slots = [2 * (y ^ k) + 1 - c for k in (0,) + LEAD]
    from_near = [[(y ^ i) == k for k in LEAD] for i in range(ys)]
    uy_rows = uy * jnp.uint32(rows)

    pair = swap(window_factor, "c", 1)
    base = jnp.concatenate([freq_factor, window_factor], axis=0)
    base, factor = lax.optimization_barrier((base, channel_factor))
    scaled = on_vmem(scale_kernel, jax.ShapeDtypeStruct(factor.shape, f32), factor).astype(f16)
    first = jnp.concatenate([base.astype(f16), scaled, pair.astype(f16)], axis=0)
    first, spectrogram, ux, xs_near, own_slots, far_slots, from_near, uy_rows = lax.optimization_barrier(
        (first, spectrogram, ux, xs_near, own_slots, far_slots, from_near, uy_rows)
    )
    first = [first] + [swap(first, "y", k) for k in LEAD]
    line = jnp.concatenate([v[freq_rows : freq_rows + 1] for v in first], axis=0)
    pair = jnp.concatenate([v[-1:] for v in first], axis=0)
    freqs = jnp.concatenate([v[:freq_rows] for v in first], axis=0).astype(bf16)
    olds = [v[freq_rows + 1 : -1].astype(f32) for v in first]
    width = win_rows * freq_rows
    half = jax.ShapeDtypeStruct((chan_rows // 2, width), bf16)
    place = pl.BlockSpec(memory_space=pltpu.VMEM)
    flat_other, flat_mine = pl.pallas_call(
        flatten_kernel,
        out_shape=(half, half),
        in_specs=[pl.BlockSpec(memory_space=pl.ANY)],
        out_specs=(place, place),
        scratch_shapes=[
            pltpu.VMEM((2, CHUNKS, rows, win_rows, freq_rows), bf16),
            pltpu.SemaphoreType.DMA((2, CHUNKS)),
        ],
        compiler_params=pltpu.CompilerParams(vmem_limit_bytes=48 * 2**20),
        cost_estimate=pl.CostEstimate(flops=0, bytes_accessed=chan_rows * width * 4, transcendentals=0),
    )(spectrogram)
    line, pair, flat_other, flat_mine = lax.optimization_barrier((line, pair, flat_other, flat_mine))
    slot = jnp.arange(win_rows)[:, None]
    block = jnp.zeros((win_rows, rank), f32)
    for i in range(ys):
        block = jnp.where(slot == own_slots[i], line[i : i + 1].astype(f32), block)
        block = jnp.where(slot == far_slots[i], pair[i : i + 1].astype(f32), block)
    half = jax.ShapeDtypeStruct((chan_rows // 2, rank), f32)
    other, khatri_rao = on_vmem(
        other_kernel, (half, jax.ShapeDtypeStruct((width, rank), bf16)), flat_other, block, freq_factor
    )
    mine = on_vmem(mine_kernel, half, flat_mine, khatri_rao)

    far = swap((other * DOWN_C).astype(f16), "c", 1).astype(f32)
    part = (mine + far * (1.0 / DOWN_C)).reshape(xs, ys * rows, rank)
    total = lax.dynamic_index_in_dim(part, ux, 0, keepdims=False)
    joined = jnp.broadcast_to(block[None], (xs, win_rows, rank))
    small = jnp.concatenate([(part * DOWN_X).astype(f16), joined.astype(f16)], axis=1)
    small, freqs = lax.optimization_barrier((small, freqs))
    pieces = [lax.dynamic_index_in_dim(small, i, 0, keepdims=False) for i in xs_near]
    pieces = [swap(v, "x", k) for v, k in zip(pieces, NEAR)]
    windows = [block.astype(bf16)] + [v[ys * rows :].astype(bf16) for v in pieces]
    two, one, three = (v[: ys * rows].astype(f32) for v in pieces)
    far = two + (one + three)
    total = total + far * (1.0 / DOWN_X)

    freqs_far = swap(freqs, "c", 1)
    total, freqs_far = lax.optimization_barrier((total, freqs_far))
    ordered = []
    for i in range(ys):
        old = olds[0]
        for v, here in zip(olds[1:], from_near[i]):
            old = jnp.where(here, v, old)
        ordered.append(old)
    like = jax.ShapeDtypeStruct((rank, ys * rows), f32)
    spread, upper, inverse = on_vmem(
        gram_kernel,
        (jax.ShapeDtypeStruct((rank, rank, rank), f32), like, like),
        freqs,
        freqs_far,
        *windows,
        jnp.concatenate(ordered, axis=0) * (1.0 / UP_U),
    )

    small = (total * DOWN_Y).astype(f16)
    two, one, three = (v.astype(f32) for v in [swap(small, "y", k) for k in NEAR])
    mttkrp = (one + three) + (small.astype(f32) + two)
    updated, squares = on_vmem(
        sweep_kernel,
        (jax.ShapeDtypeStruct((ys * rows, rank), f32), jax.ShapeDtypeStruct((1, rank), f32)),
        mttkrp,
        spread,
        upper,
        inverse,
    )
    updated = lax.dynamic_slice_in_dim(updated, uy_rows, rows, 0)
    squares = squares + swap(squares, "c", 1)
    lines = xs * lax.axis_size("z")
    updated, squares = lax.optimization_barrier((updated, squares))
    order = [[(i + lines * 11 // 16) % lines for i in range(lines)]]
    squares = lax.all_to_all(
        jnp.broadcast_to(squares, (lines, rank)), ("z", "x"), 0, 0, tiled=True, axis_index_groups=order
    ).sum(axis=0)
    column_scale = jnp.sqrt(squares / (lines * 2 * ys * rows) + 1e-06)
    return (updated / column_scale[None, :], column_scale)


def solution(mesh):
    chan, win, freq = mesh.devices.shape
    fine = Mesh(mesh.devices.reshape(chan, win, freq // 2, 2), ("z", "x", "y", "c"))
    placed = (
        P("z", "x", ("y", "c")),
        P(("x", "y", "c"), None),
        P(("y", "c"), None),
        P(("z", "x", "y", "c"), None),
    )
    return jax.shard_map(
        body,
        mesh=fine,
        in_specs=placed,
        out_specs=(P(("z", "x", "y", "c"), None), P()),
        check_vma=False,
    )
```
